32 devices in a mesh: rec: 2 (over x), row: 4 (over y, core), col: 4 (over z).
Axes of the slice: x: 2, y: 2, z: 4, core: 2. Of those that a mesh axis runs over, the one named last changes fastest.
Arguments:
- local_derivs: bfloat16 [64, 256, 128], P(('rec', 'row', 'col')), may hold values from -6 to 6
- global_derivs: bfloat16 [64, 256, 384], P(('rec', 'row', 'col')), may hold values from -64 to 64
- weights: float32 [64, 256], P(('rec', 'row', 'col')), may hold values from 0.25 to 4
- first_block: int32 [64], P(('rec', 'row', 'col')), may hold values from 0 to 6
- bundle_count: int32 [32], P(('rec', 'row', 'col')), may hold values from 1 to 2
- trailing_block: float32 [2048, 2048], P(('rec', 'row'), 'col'), may hold values from -6 to 6
Outputs:
- updated: float32 [2048, 2048], P(('rec', 'row'), 'col')
The draws below stay inside these ranges and needn't reach their ends.
All inputs are finite; a program needn't handle non-finite values.
Results may differ from the reference program's by a relative error of at most 0.0094.
Values may be sent and summed in bfloat16 or wider, within the bound.
No kernel may reach another device: no remote copies, remote signals or barrier semaphores. Data moves between devices by JAX's collectives and lax.ppermute only.
A program may use at most 64 MiB of HBM per device.

```python
import math
import jax
import jax.numpy as jnp
from jax import lax

BLK = 128
LOCAL = 128
PBLK = 8
ROWS = 256
NBD = 2
TRAIL = 2048
BUNDLES = 64
N_REC = 2
N_ROW = 4
N_COL = 4
DEVICES = 32


def draw_global_derivs(key, part):
    base_key = jax.random.fold_in(key, 7101)
    noise_key = jax.random.fold_in(key, 7102)
    scale_key = jax.random.fold_in(key, 7103)
    full_shape = (BUNDLES, ROWS, 3 * BLK)
    base = 1.3 * jax.random.normal(base_key, full_shape, jnp.float32)
    fresh = 1.3 * jax.random.normal(noise_key, (BUNDLES, ROWS, BLK), jnp.float32)
    first_part = base[:, :, :BLK]
    second_part = 0.9 * first_part + 0.44 * fresh
    trail_part = base[:, :, 2 * BLK:]
    upper = jnp.float32(math.log(16.0))
    spread = jax.random.uniform(scale_key, (BLK,), jnp.float32, 0.0, 1.0) * upper
    scales = 16.0 * jnp.exp(spread - jnp.max(spread))
    scales = jnp.maximum(scales, 1.0)
    first_part = jnp.clip(first_part, -4.0, 4.0) * scales
    second_part = jnp.clip(second_part, -4.0, 4.0) * scales
    trail_part = jnp.clip(trail_part, -4.0, 4.0)
    whole = jnp.concatenate([first_part, second_part, trail_part], axis=2)
    return whole.astype(jnp.bfloat16)


def plant(array, rng, least, largest):
    longest = array.shape.index(max(array.shape))
    spots = []
    for shift in (0, 1):
        where = [jax.random.randint(jax.random.fold_in(rng, axis), (), 0, length) for axis, length in enumerate(array.shape)]
        where[longest] = (where[longest] + shift) % array.shape[longest]
        spots.append(tuple(where))
    return array.at[spots[0]].set(least).at[spots[1]].set(largest)


def level_of(rng, extent, cuts, low, largest):
    gain, own = 1.0, jax.random.fold_in(rng, 6)
    for dim, blocks in cuts:
        steps = jnp.exp(jax.random.uniform(jax.random.fold_in(own, dim), (blocks,), jnp.float32, low / len(cuts), largest / len(cuts)))
        gain = gain * jnp.repeat(steps, extent[dim] // blocks).reshape([-1 if axis == dim else 1 for axis in range(len(extent))])
    return gain


def normal_values(stream_key, shape, deviation, bound, cuts=(), kind=jnp.bfloat16):
    array = jax.random.normal(stream_key, shape, jnp.float32) * deviation
    if len(cuts) > 0:
        array = level_of(stream_key, shape, cuts, -0.22, 0.18) * array
    return jnp.clip(array, min=-bound, max=bound).astype(kind)


def setup_inputs(seed: int = 0) -> dict:
    key_list = jax.random.split(jax.random.key(seed), 7)
    local_derivs = normal_values(key_list[0], (BUNDLES, ROWS, LOCAL), 1.0, 6.0, ((0, 32),))
    global_derivs = draw_global_derivs(jax.random.fold_in(key_list[6], 71), 0)
    weights = jnp.clip(jnp.exp(math.log(4.0) - 2.7725887 * jax.random.uniform(key_list[2], (BUNDLES, ROWS), jnp.float32) ** level_of(key_list[2], (BUNDLES, ROWS), ((0, 32),), -0.2, 0.2)), 0.25, 4.0)
    first_block = plant(jax.random.randint(key_list[3], (BUNDLES,), 0, PBLK - 1), jax.random.fold_in(key_list[3], 1), 0, (PBLK - 1) - 1).astype(jnp.int32)
    bundle_count = plant(jax.random.randint(key_list[4], (DEVICES,), 1, NBD + 1), jax.random.fold_in(key_list[4], 1), 1, NBD).astype(jnp.int32)
    trailing_block = normal_values(key_list[5], (TRAIL, TRAIL), 1.0, 6.0, ((0, 8), (1, 4)), jnp.float32)
    return dict(local_derivs=local_derivs, global_derivs=global_derivs, weights=weights, first_block=first_block, bundle_count=bundle_count, trailing_block=trailing_block)


HIGH = lax.Precision.HIGHEST

def invert_lower(factor):
    eye = jnp.eye(factor.shape[-1], dtype=factor.dtype)
    eye = jnp.broadcast_to(eye, factor.shape)
    return lax.linalg.triangular_solve(factor, eye, left_side=True, lower=True)

def bundle_terms(local_derivs, global_derivs, weights, first_block, live):
    root = jnp.sqrt(weights)[:, :, None]
    scaled_local = (root * local_derivs.astype(jnp.float32)).astype(jnp.bfloat16).astype(jnp.float32)
    scaled_global = (root * global_derivs.astype(jnp.float32)).astype(jnp.bfloat16).astype(jnp.float32)
    local_gram = jnp.einsum('nrl,nrm->nlm', scaled_local, scaled_local, precision=HIGH)
    cross_gram = jnp.einsum('nrg,nrl->ngl', scaled_global, scaled_local, precision=HIGH)
    panel_gram = jnp.einsum('nra,nrg->nag', scaled_global[:, :, :2 * BLK], scaled_global, precision=HIGH)
    local_inverse = invert_lower(jnp.linalg.cholesky(local_gram))
    whitened = jnp.einsum('nlm,ngm->nlg', local_inverse, cross_gram, precision=HIGH)
    reduced = panel_gram - jnp.einsum('nla,nlg->nag', whitened[:, :, :2 * BLK], whitened, precision=HIGH)
    reduced = reduced * live[:, None, None]
    marks = jnp.arange(PBLK, dtype=jnp.int32)
    first_hot = (first_block[:, None] == marks[None, :]).astype(jnp.float32)
    second_hot = (first_block[:, None] + 1 == marks[None, :]).astype(jnp.float32)
    diag_part = jnp.einsum('nk,nab->kab', first_hot, reduced[:, :BLK, :BLK], precision=HIGH)
    diag_part = diag_part + jnp.einsum('nk,nab->kab', second_hot, reduced[:, BLK:2 * BLK, BLK:2 * BLK], precision=HIGH)
    sub_part = jnp.einsum('nk,nab->kab', second_hot, reduced[:, BLK:2 * BLK, :BLK], precision=HIGH)
    panel_part = jnp.einsum('nk,nab->kab', first_hot, reduced[:, :BLK, 2 * BLK:], precision=HIGH)
    panel_part = panel_part + jnp.einsum('nk,nab->kab', second_hot, reduced[:, BLK:2 * BLK, 2 * BLK:], precision=HIGH)
    return (jnp.stack([diag_part, sub_part], axis=1), panel_part.reshape(PBLK * BLK, BLK))

def step_block(diag, sub, panel_rows, inv_prev, sol_prev):
    low = jnp.dot(sub, inv_prev.T, precision=HIGH)
    inverse = invert_lower(jnp.linalg.cholesky(diag - jnp.dot(low, low.T, precision=HIGH)))
    solved = jnp.dot(inverse, panel_rows - jnp.dot(low, sol_prev, precision=HIGH), precision=HIGH)
    return (inverse, solved)

def reference(local_derivs, global_derivs, weights, first_block, bundle_count, trailing_block):
    shards = N_REC * N_ROW * N_COL
    stretches = N_ROW * N_COL
    local_split = local_derivs.reshape(shards, NBD, ROWS, LOCAL)
    global_split = global_derivs.reshape(shards, NBD, ROWS, 3 * BLK)
    weight_split = weights.reshape(shards, NBD, ROWS)
    first_split = first_block.reshape(shards, NBD)

    def visit(carry, items):
        block_total, panel = carry
        loc, glo, wts, first, count, shard = items
        live = (jnp.arange(NBD, dtype=jnp.int32) < count).astype(jnp.float32)
        stacked, panel_part = bundle_terms(loc, glo, wts, first, live)
        column = (shard % stretches * BLK).astype(jnp.int32)
        current = lax.dynamic_slice_in_dim(panel, column, BLK, 1)
        panel = lax.dynamic_update_slice_in_dim(panel, current + panel_part, column, 1)
        return ((block_total + stacked, panel), None)
    start = (jnp.zeros((PBLK, 2, BLK, BLK), jnp.float32), jnp.zeros((PBLK * BLK, TRAIL), jnp.float32))
    items = (local_split, global_split, weight_split, first_split, bundle_count, jnp.arange(shards, dtype=jnp.int32))
    (blocks, panel), _ = lax.scan(visit, start, items)
    inv_prev = jnp.eye(BLK, dtype=jnp.float32)
    sol_prev = jnp.zeros((BLK, TRAIL), jnp.float32)
    pieces = []
    for index in range(PBLK):
        rows = panel[index * BLK:(index + 1) * BLK]
        inv_prev, sol_prev = step_block(blocks[index, 0], blocks[index, 1], rows, inv_prev, sol_prev)
        pieces.append(sol_prev)
    solved_low = jnp.concatenate(pieces, axis=0).astype(jnp.bfloat16)
    update = lax.dot_general(solved_low.astype(jnp.float32), solved_low.astype(jnp.float32), (((0,), (0,)), ((), ())), preferred_element_type=jnp.float32)
    return trailing_block - update
```

```python
import functools

import jax
import jax.numpy as jnp
from jax import lax
from jax.experimental import pallas as pl
from jax.experimental.pallas import tpu as pltpu
from jax.sharding import PartitionSpec as P

PBLK = 8
AXES = ("rec", "row", "col")
F32 = jnp.float32
BF16 = jnp.bfloat16
SUB = 8
VMEM_BYTES = 40 * 1024 * 1024

ROWS_BY_ROWS = (((0,), (0,)), ((), ()))
COLS_BY_COLS = (((1,), (1,)), ((), ()))
PLAIN = (((1,), (0,)), ((), ()))


def split(x):
    if x.dtype == BF16:
        return x, None
    high = x.astype(BF16)
    return high, (x - high.astype(F32)).astype(BF16)


def dot3(a, b, dims):
    a_high, a_low = split(a)
    b_high, b_low = split(b)
    mul = functools.partial(lax.dot_general, dimension_numbers=dims, preferred_element_type=F32)
    out = mul(a_high, b_high)
    if b_low is not None:
        out = out + mul(a_high, b_low)
    if a_low is not None:
        out = out + mul(a_low, b_high)
    return out


def lane_copy(x, at, size):
    return jnp.broadcast_to(x[:, at : at + 1], (SUB, size))


def row_copy(x, at, size):
    return jnp.broadcast_to(x[at : at + 1, :], (SUB, size))


def factor_step(rows, step, lane, sub):
    size = lane.shape[1]
    first = step * SUB
    inside = (lane >= first) & (lane < first + SUB)
    pivot_rows = [row_copy(rows[step], i, size) for i in range(SUB)]
    entry = {
        (i, j): lane_copy(pivot_rows[i], first + j, size) for i in range(SUB) for j in range(i, SUB)
    }
    below = range(step + 1, len(rows))
    cols = {r: [lane_copy(rows[r], first + j, size) for j in range(SUB)] for r in below}
    left = [
        jnp.where(inside, jnp.where(lane == first + i, 1.0, 0.0), pivot_rows[i]) for i in range(SUB)
    ]
    recip = [None] * SUB
    mult = {}
    for k in range(SUB):
        recip[k] = 1.0 / entry[(k, k)]
        for i in range(k + 1, SUB):
            mult[(i, k)] = entry[(k, i)] * recip[k]
        for i in range(k + 1, SUB):
            for j in range(i, SUB):
                entry[(i, j)] = entry[(i, j)] - mult[(i, k)] * entry[(k, j)]
            left[i] = left[i] - mult[(i, k)] * left[k]
    solved = [left[i] * recip[i] for i in range(SUB)]
    done = left[0] * lax.sqrt(recip[0])
    for i in range(1, SUB):
        done = jnp.where(sub == i, left[i] * lax.sqrt(recip[i]), done)
    for k in range(SUB - 1, 0, -1):
        for i in range(k):
            solved[i] = solved[i] - mult[(k, i)] * solved[k]
    for r in below:
        part = [cols[r][j] * solved[j] for j in range(SUB)]
        while len(part) > 1:
            part = [part[i] + part[i + 1] for i in range(0, len(part), 2)]
        rows[r] = jnp.where(inside, 0.0, rows[r]) - part[0]
    rows[step] = jnp.where(lane < first + SUB, done, 0.0)


def inverse_factors(mats):
    size = mats[0].shape[0]
    lane = lax.broadcasted_iota(jnp.int32, (SUB, size), 1)
    sub = lax.broadcasted_iota(jnp.int32, (SUB, size), 0)
    state = [[m[r : r + SUB, :] for r in range(0, size, SUB)] for m in mats]
    for step in range(size // SUB):
        for rows in state:
            factor_step(rows, step, lane, sub)
    return [jnp.concatenate(rows, axis=0) for rows in state]


def local_kernel(
    me, pan, first_ref, count_ref, local_ref, global_ref, weight_ref,
    keep_ref, send_ref, pkeep_ref, psend_ref, tri, panel,
):
    slots = local_ref.shape[0]
    block = local_ref.shape[2]
    tri[...] = jnp.zeros_like(tri)
    panel[...] = jnp.zeros_like(panel)
    root = jnp.sqrt(weight_ref[...])
    root = jnp.transpose(jnp.concatenate([root] * (SUB // slots), axis=0))
    grams, crosses, panels = [], [], []
    for b in range(slots):
        col = root[:, b : b + 1]
        loc = (col * local_ref[b].astype(F32)).astype(BF16)
        glo = (col * global_ref[b].astype(F32)).astype(BF16)
        dot = functools.partial(
            lax.dot_general, dimension_numbers=ROWS_BY_ROWS, preferred_element_type=F32
        )
        grams.append(dot(loc, loc))
        crosses.append(dot(loc, glo))
        panels.append(dot(glo[:, : 2 * block], glo))
    inverses = inverse_factors(grams)
    for b in range(slots):
        white = dot3(inverses[b], crosses[b], PLAIN)
        reduced = panels[b] - dot3(white[:, : 2 * block], white, ROWS_BY_ROWS)
        live = jnp.where(count_ref[0] > b, 1.0, 0.0)
        reduced = reduced * live
        k = first_ref[b]
        one = lax.bitwise_xor(k, me)
        two = lax.bitwise_xor(k + 1, me)
        tri[one, 0] += reduced[:block, :block]
        tri[two, 0] += reduced[block:, block : 2 * block]
        tri[two, 1] += reduced[block:, :block]
        panel[lax.bitwise_xor(k, pan)] += reduced[:block, 2 * block :]
        panel[lax.bitwise_xor(k + 1, pan)] += reduced[block:, 2 * block :]
    half = PBLK // 2
    for j in range(half):
        keep_ref[j] = tri[2 * j]
        send_ref[j] = tri[2 * j + 1]
    pkeep_ref[...] = panel[:half]
    psend_ref[...] = panel[half:].astype(BF16)


def add_kernel(a_ref, b_ref, *out_refs):
    for j, ref in enumerate(out_refs):
        ref[...] = a_ref[j] + b_ref[j]


def levels_of(count):
    left = list(range(count))
    levels = []
    while left:
        gone = left[0::2] if len(left) > 1 else left
        level = []
        for k in gone:
            at = left.index(k)
            before = left[at - 1] if at > 0 else None
            after = left[at + 1] if at + 1 < len(left) else None
            level.append((k, before, after))
        levels.append(level)
        left = [k for k in left if k not in gone]
    return levels


def couplings_of(count):
    return [
        (k, n, side)
        for level in levels_of(count)
        for k, before, after in level
        for n, side in ((before, "before"), (after, "after"))
        if n is not None
    ]


def chain_kernel(me, *refs):
    pieces = refs[:PBLK]
    inv_ref, low_ref, tri = refs[PBLK:]
    for j in range(PBLK):
        tri[lax.bitwise_xor(me, j)] = pieces[j][...]
    diag = {k: tri[k, 0] for k in range(PBLK)}
    off = {(k, k - 1): tri[k, 1] for k in range(1, PBLK)}
    slot = {key[:2]: i for i, key in enumerate(couplings_of(PBLK))}
    for level in levels_of(PBLK):
        inverses = inverse_factors([diag[k] for k, _, _ in level])
        for (k, before, after), inv in zip(level, inverses):
            inv_ref[k] = inv
            if before is not None:
                low_b = dot3(inv, off[(k, before)], PLAIN)
                low_ref[slot[(k, before)]] = low_b
                diag[before] = diag[before] - dot3(low_b, low_b, ROWS_BY_ROWS)
            if after is not None:
                low_a = dot3(off[(after, k)], inv, COLS_BY_COLS)
                low_ref[slot[(k, after)]] = low_a
                diag[after] = diag[after] - dot3(low_a, low_a, COLS_BY_COLS)
            if before is not None and after is not None:
                off[(after, before)] = -dot3(low_a, low_b, PLAIN)


def final_kernel(col_me, n_rec, inv_ref, low_ref, pc_ref, *refs):
    n_col = len(refs) - 4
    rows_refs = refs[:n_col]
    trail_ref, out_ref, panel, solved = refs[n_col:]
    height, block = rows_refs[0].shape
    tile_rows = trail_ref.shape[0]
    n_row = pc_ref.shape[0] // n_rec
    for r in range(n_rec):
        for i in range(n_row):
            at = tile_rows + i * block
            panel[r * height : (r + 1) * height, at : at + block] = pc_ref[r * n_row + i]
    for m in range(n_col):
        q = lax.bitwise_xor(col_me, m)
        down = pl.multiple_of(lax.rem(q, n_rec) * height, height)
        over = pl.multiple_of(lax.div(q, n_rec) * block, block)
        panel[pl.ds(down, height), pl.ds(over, block)] = rows_refs[m][...]
    slot = {key[:2]: i for i, key in enumerate(couplings_of(PBLK))}
    value = {k: panel[k * block : (k + 1) * block, :] for k in range(PBLK)}
    for level in levels_of(PBLK):
        for k, before, after in level:
            sol = dot3(inv_ref[k], value[k], PLAIN)
            solved[k * block : (k + 1) * block, :] = sol.astype(BF16)
            if before is not None:
                low_b = low_ref[slot[(k, before)]]
                value[before] = value[before].astype(F32) - dot3(low_b, sol, ROWS_BY_ROWS)
            if after is not None:
                low_a = low_ref[slot[(k, after)]]
                value[after] = value[after].astype(F32) - dot3(low_a, sol, PLAIN)
    update = lax.dot_general(
        solved[:, :tile_rows], solved[:, tile_rows:], ROWS_BY_ROWS, preferred_element_type=F32
    )
    out_ref[...] = trail_ref[...] - update


VMEM = pl.BlockSpec(memory_space=pltpu.VMEM)
SMEM = pl.BlockSpec(memory_space=pltpu.SMEM)
PARAMS = pltpu.CompilerParams(vmem_limit_bytes=VMEM_BYTES)


def call(kernel, out_shape, ins, scratch=(), scalars=0):
    return pl.pallas_call(
        kernel,
        out_shape=out_shape,
        in_specs=[SMEM] * scalars + [VMEM] * (len(ins) - scalars),
        out_specs=jax.tree.map(lambda _: VMEM, out_shape),
        scratch_shapes=scratch,
        compiler_params=PARAMS,
    )(*ins)


def flipped(x, mask, count):
    return lax.ppermute(x, AXES, [(i, i ^ mask) for i in range(count)])


def body(local_derivs, global_derivs, weights, first_block, bundle_count, trailing_block):
    n_rec, n_row, n_col = (lax.axis_size(a) for a in AXES)
    count = n_rec * n_row * n_col
    rec, row, col = (lax.axis_index(a) for a in AXES)
    block = local_derivs.shape[2]
    half = PBLK // 2
    low_rec = PBLK // n_row
    me = row + n_row * lax.rem(rec, low_rec)
    pan = rec * half if n_rec == 2 else jnp.int32(0)
    ids = jnp.stack([me, pan, col]).astype(jnp.int32)
    shape = jax.ShapeDtypeStruct

    def local_body(ids_ref, *refs):
        local_kernel(ids_ref[0], ids_ref[1], *refs)

    keep, send, pkeep, psend = call(
        local_body,
        [
            shape((half, 2, block, block), F32),
            shape((half, 2, block, block), F32),
            shape((half, block, block), F32),
            shape((half, block, block), BF16),
        ],
        [ids, first_block, bundle_count, local_derivs, global_derivs, weights],
        [pltpu.VMEM((PBLK, 2, block, block), F32), pltpu.VMEM((PBLK, block, block), F32)],
        scalars=3,
    )
    got = flipped(send, n_col, count)
    if n_rec == 2:
        pgot = flipped(psend, n_row * n_col, count)
        height = half * block
        pmine = (pkeep + pgot.astype(F32)).astype(BF16).reshape(height, block)
    else:
        whole = jnp.concatenate([pkeep, psend.astype(F32)], axis=0).reshape(PBLK * block, block)
        pmine = lax.psum_scatter(whole, "rec", scatter_dimension=0, tiled=True).astype(BF16)
        height = pmine.shape[0]
    pieces = call(add_kernel, [shape((2, block, block), F32)] * half, [keep, got])
    total = pieces[0]
    for j in range(1, half):
        total = total + flipped(pieces[j], 2 * j * n_col, count)
    for bit in range(1, n_rec // low_rec):
        if bit & (bit - 1) == 0:
            total = total + flipped(total, bit * low_rec * n_row * n_col, count)
    if n_col <= 4:
        total = sum((flipped(total, m, count) for m in range(1, n_col)), total)
    else:
        total = lax.psum(total, "col")
    evens = [total] + [flipped(total, 2 * j * n_col, count) for j in range(1, half)]
    odds = [flipped(x, n_col, count) for x in evens]
    tri = [x for pair in zip(evens, odds) for x in pair]

    owner = lambda r, c: (r * n_row + c // n_col) * n_col + c % n_col
    device = lambda r, i, j: (r * n_row + i) * n_col + j
    grid = [(r, i, j) for r in range(n_rec) for i in range(n_row) for j in range(n_col)]
    to_cols = [(owner(r, n_row * j + i), device(r, i, j)) for r, i, j in grid]
    per = n_col // n_rec
    to_rows = [
        (owner(j % n_rec, (r * n_row + i) * per + j // n_rec), device(r, i, j)) for r, i, j in grid
    ]
    pcols = lax.all_gather(lax.ppermute(pmine, AXES, to_cols), ("rec", "row"), axis=0)
    prows = lax.ppermute(pmine, AXES, to_rows)
    if n_col <= 4:
        prows = [prows] + [flipped(prows, m, count) for m in range(1, n_col)]
        col_key = col
    else:
        every = lax.all_gather(prows, "col", axis=0)
        prows = [every[m] for m in range(n_col)]
        col_key = jnp.int32(0)

    inverses, lows = call(
        lambda ids_ref, *refs: chain_kernel(ids_ref[0], *refs),
        [
            shape((PBLK, block, block), F32),
            shape((len(couplings_of(PBLK)), block, block), F32),
        ],
        [ids, *tri],
        [pltpu.VMEM((PBLK, 2, block, block), F32)],
        scalars=1,
    )
    wide = trailing_block.shape[0] + trailing_block.shape[1]
    key = jnp.reshape(col_key, (1,)).astype(jnp.int32)
    return call(
        lambda key_ref, *refs: final_kernel(key_ref[0], n_rec, *refs),
        shape(trailing_block.shape, F32),
        [key, inverses, lows, pcols, *prows, trailing_block],
        [pltpu.VMEM((PBLK * block, wide), BF16), pltpu.VMEM((PBLK * block, wide), BF16)],
        scalars=1,
    )


def solution(mesh):
    return jax.shard_map(
        body,
        mesh=mesh,
        in_specs=(
            P(("rec", "row", "col"), None, None),
            P(("rec", "row", "col"), None, None),
            P(("rec", "row", "col"), None),
            P(("rec", "row", "col")),
            P(("rec", "row", "col")),
            P(("rec", "row"), "col"),
        ),
        out_specs=P(("rec", "row"), "col"),
        check_vma=False,
    )
```

```python
import functools

import jax
import jax.numpy as jnp
from jax import lax
from jax.experimental import pallas as pl
from jax.experimental.pallas import tpu as pltpu
from jax.sharding import PartitionSpec as P

PBLK = 8
AXES = ("rec", "row", "col")
F32 = jnp.float32
BF16 = jnp.bfloat16
SUB = 8
TAIL = 16
VMEM_BYTES = 40 * 1024 * 1024

ROWS_BY_ROWS = (((0,), (0,)), ((), ()))
COLS_BY_COLS = (((1,), (1,)), ((), ()))
PLAIN = (((1,), (0,)), ((), ()))


def split(x):
    if x.dtype == BF16:
        return x, None
    high = x.astype(BF16)
    return high, (x - high.astype(F32)).astype(BF16)


def dot3(a, b, dims):
    a_high, a_low = split(a)
    b_high, b_low = split(b)
    mul = functools.partial(lax.dot_general, dimension_numbers=dims, preferred_element_type=F32)
    out = mul(a_high, b_high)
    if b_low is not None:
        out = out + mul(a_high, b_low)
    if a_low is not None:
        out = out + mul(a_low, b_high)
    return out


def lane_copy(x, at, size):
    return jnp.broadcast_to(x[:, at : at + 1], (SUB, size))


def row_copy(x, at, size):
    return jnp.broadcast_to(x[at : at + 1, :], (SUB, size))


def factor_step(rows, step, lane, sub):
    size = lane.shape[1]
    first = step * SUB
    inside = (lane >= first) & (lane < first + SUB)
    pivot_rows = [row_copy(rows[step], i, size) for i in range(SUB)]
    entry = {
        (i, j): lane_copy(pivot_rows[i], first + j, size) for i in range(SUB) for j in range(i, SUB)
    }
    below = range(step + 1, len(rows))
    cols = {r: [lane_copy(rows[r], first + j, size) for j in range(SUB)] for r in below}
    left = [
        jnp.where(inside, jnp.where(lane == first + i, 1.0, 0.0), pivot_rows[i]) for i in range(SUB)
    ]
    recip = [None] * SUB
    mult = {}
    for k in range(SUB):
        recip[k] = 1.0 / entry[(k, k)]
        for i in range(k + 1, SUB):
            mult[(i, k)] = entry[(k, i)] * recip[k]
        for i in range(k + 1, SUB):
            for j in range(i, SUB):
                entry[(i, j)] = entry[(i, j)] - mult[(i, k)] * entry[(k, j)]
            left[i] = left[i] - mult[(i, k)] * left[k]
    solved = [left[i] * recip[i] for i in range(SUB)]
    done = left[0] * lax.sqrt(recip[0])
    for i in range(1, SUB):
        done = jnp.where(sub == i, left[i] * lax.sqrt(recip[i]), done)
    for k in range(SUB - 1, 0, -1):
        for i in range(k):
            solved[i] = solved[i] - mult[(k, i)] * solved[k]
    for r in below:
        part = [cols[r][j] * solved[j] for j in range(SUB)]
        while len(part) > 1:
            part = [part[i] + part[i + 1] for i in range(0, len(part), 2)]
        rows[r] = jnp.where(inside, 0.0, rows[r]) - part[0]
    rows[step] = jnp.where(lane < first + SUB, done, 0.0)


def inverse_factors(mats):
    size = mats[0].shape[0]
    lane = lax.broadcasted_iota(jnp.int32, (SUB, size), 1)
    sub = lax.broadcasted_iota(jnp.int32, (SUB, size), 0)
    state = [[m[r : r + SUB, :] for r in range(0, size, SUB)] for m in mats]
    for step in range(size // SUB):
        for rows in state:
            factor_step(rows, step, lane, sub)
    return [jnp.concatenate(rows, axis=0) for rows in state]


def local_kernel(
    me, first_ref, count_ref, local_hbm, global_hbm, weight_hbm,
    keep_ref, send_ref, piece_ref, tri, local_ref, global_ref, weight_ref, sems,
):
    copies = [
        pltpu.make_async_copy(src, dst, sems.at[i])
        for i, (src, dst) in enumerate(
            [(weight_hbm, weight_ref), (local_hbm, local_ref), (global_hbm, global_ref)]
        )
    ]
    for copy in copies:
        copy.start()
    slots = local_ref.shape[0]
    block = local_ref.shape[2]
    tri[...] = jnp.zeros_like(tri)
    dot = functools.partial(
        lax.dot_general, dimension_numbers=ROWS_BY_ROWS, preferred_element_type=F32
    )
    copies[0].wait()
    root = jnp.sqrt(weight_ref[...])
    root = jnp.transpose(jnp.concatenate([root] * (SUB // slots), axis=0))
    copies[1].wait()
    cols = [root[:, b : b + 1] for b in range(slots)]
    locs = [(cols[b] * local_ref[b].astype(F32)).astype(BF16) for b in range(slots)]
    grams = [dot(loc, loc) for loc in locs]
    copies[2].wait()
    crosses, panels = [], []
    for b in range(slots):
        glo = (cols[b] * global_ref[b].astype(F32)).astype(BF16)
        crosses.append(dot(locs[b], glo))
        panels.append(dot(glo[:, : 2 * block], glo))
    inverses = inverse_factors(grams)
    for b in range(slots):
        white = dot3(inverses[b], crosses[b], PLAIN)
        reduced = panels[b] - dot3(white[:, : 2 * block], white, ROWS_BY_ROWS)
        live = jnp.where(count_ref[0] > b, 1.0, 0.0)
        reduced = reduced * live
        k = first_ref[b]
        one = lax.bitwise_xor(k, me)
        two = lax.bitwise_xor(k + 1, me)
        tri[one, 0] += reduced[:block, :block]
        tri[two, 0] += reduced[block:, block : 2 * block]
        tri[two, 1] += reduced[block:, :block]
        piece_ref[b, : 2 * block, :] = reduced[:, 2 * block :].astype(BF16)
        tail = jnp.broadcast_to(k.astype(F32), (TAIL, block))
        piece_ref[b, 2 * block :, :] = tail.astype(BF16)
    half = PBLK // 2
    for j in range(half):
        keep_ref[j] = tri[2 * j]
        send_ref[j] = tri[2 * j + 1]


def add_kernel(a_ref, b_ref, *out_refs):
    for j, ref in enumerate(out_refs):
        ref[...] = a_ref[j] + b_ref[j]


def levels_of(count):
    left = list(range(count))
    levels = []
    while left:
        gone = left[0::2] if len(left) > 1 else left
        level = []
        for k in gone:
            at = left.index(k)
            before = left[at - 1] if at > 0 else None
            after = left[at + 1] if at + 1 < len(left) else None
            level.append((k, before, after))
        levels.append(level)
        left = [k for k in left if k not in gone]
    return levels


def couplings_of(count):
    return [
        (k, n, side)
        for level in levels_of(count)
        for k, before, after in level
        for n, side in ((before, "before"), (after, "after"))
        if n is not None
    ]


def chain_kernel(me, *refs):
    pieces = refs[:PBLK]
    inv_ref, low_ref, tri = refs[PBLK:]
    for j in range(PBLK):
        tri[lax.bitwise_xor(me, j)] = pieces[j][...]
    diag = {k: tri[k, 0] for k in range(PBLK)}
    off = {(k, k - 1): tri[k, 1] for k in range(1, PBLK)}
    slot = {key[:2]: i for i, key in enumerate(couplings_of(PBLK))}
    for level in levels_of(PBLK):
        inverses = inverse_factors([diag[k] for k, _, _ in level])
        for (k, before, after), inv in zip(level, inverses):
            inv_ref[k] = inv
            if before is not None:
                low_b = dot3(inv, off[(k, before)], PLAIN)
                low_ref[slot[(k, before)]] = low_b
                diag[before] = diag[before] - dot3(low_b, low_b, ROWS_BY_ROWS)
            if after is not None:
                low_a = dot3(off[(after, k)], inv, COLS_BY_COLS)
                low_ref[slot[(k, after)]] = low_a
                diag[after] = diag[after] - dot3(low_a, low_a, COLS_BY_COLS)
            if before is not None and after is not None:
                off[(after, before)] = -dot3(low_a, low_b, PLAIN)


def final_kernel(cols_me, rows_me, n_row, per, n_cols, inv_ref, low_ref, *refs):
    terms, (trail_ref, out_ref, panel, solved) = refs[:-4], refs[-4:]
    slots, height, block = terms[0].shape
    height = height - TAIL
    tile_rows = trail_ref.shape[0]
    panel[...] = jnp.zeros_like(panel)
    for n, term in enumerate(terms):
        if n < n_cols:
            over = tile_rows + lax.rem(lax.bitwise_xor(cols_me, n), n_row) * block
        else:
            over = lax.rem(lax.bitwise_xor(rows_me, n - n_cols), per) * block
        over = pl.multiple_of(over, block)
        for b in range(slots):
            k = jnp.max(term[b, height:, :].astype(F32)).astype(jnp.int32)
            down = pl.multiple_of(k * block, block)
            panel[pl.ds(down, height), pl.ds(over, block)] += term[b, :height, :].astype(F32)
    slot = {key[:2]: i for i, key in enumerate(couplings_of(PBLK))}
    value = {k: panel[k * block : (k + 1) * block, :] for k in range(PBLK)}
    for level in levels_of(PBLK):
        for k, before, after in level:
            sol = dot3(inv_ref[k], value[k], PLAIN)
            solved[k * block : (k + 1) * block, :] = sol.astype(BF16)
            if before is not None:
                low_b = low_ref[slot[(k, before)]]
                value[before] = value[before] - dot3(low_b, sol, ROWS_BY_ROWS)
            if after is not None:
                low_a = low_ref[slot[(k, after)]]
                value[after] = value[after] - dot3(low_a, sol, PLAIN)
    update = lax.dot_general(
        solved[:, :tile_rows], solved[:, tile_rows:], ROWS_BY_ROWS, preferred_element_type=F32
    )
    out_ref[...] = trail_ref[...] - update


VMEM = pl.BlockSpec(memory_space=pltpu.VMEM)
SMEM = pl.BlockSpec(memory_space=pltpu.SMEM)
HBM = pl.BlockSpec(memory_space=pltpu.HBM)
PARAMS = pltpu.CompilerParams(vmem_limit_bytes=VMEM_BYTES)


def call(kernel, out_shape, ins, scratch=(), scalars=0, hbm=()):
    return pl.pallas_call(
        kernel,
        out_shape=out_shape,
        in_specs=[SMEM if i < scalars else HBM if i in hbm else VMEM for i in range(len(ins))],
        out_specs=jax.tree.map(lambda _: VMEM, out_shape),
        scratch_shapes=scratch,
        compiler_params=PARAMS,
    )(*ins)


def after(x, *others):
    return lax.optimization_barrier((x, others))[0]


def flipped(x, mask, count):
    return lax.ppermute(x, AXES, [(i, i ^ mask) for i in range(count)])


def body(local_derivs, global_derivs, weights, first_block, bundle_count, trailing_block):
    n_rec, n_row, n_col = (lax.axis_size(a) for a in AXES)
    count = n_rec * n_row * n_col
    rec, row, col = (lax.axis_index(a) for a in AXES)
    block = local_derivs.shape[2]
    half = PBLK // 2
    low_rec = PBLK // n_row
    me = row + n_row * lax.rem(rec, low_rec)
    ids = jnp.reshape(me, (1,)).astype(jnp.int32)
    shape = jax.ShapeDtypeStruct
    slots, height = local_derivs.shape[0], 2 * block + TAIL
    keep, send, piece = call(
        lambda ids_ref, *refs: local_kernel(ids_ref[0], *refs),
        [
            shape((half, 2, block, block), F32),
            shape((half, 2, block, block), F32),
            shape((slots, height, block), BF16),
        ],
        [ids, first_block, bundle_count, local_derivs, global_derivs, weights],
        [
            pltpu.VMEM((PBLK, 2, block, block), F32),
            pltpu.VMEM(local_derivs.shape, BF16),
            pltpu.VMEM(global_derivs.shape, BF16),
            pltpu.VMEM(weights.shape, F32),
            pltpu.SemaphoreType.DMA((3,)),
        ],
        scalars=3,
        hbm=(3, 4, 5),
    )
    per = n_col // n_rec
    owner = lambda r, c: (r * n_row + c // n_col) * n_col + c % n_col
    device = lambda r, i, j: (r * n_row + i) * n_col + j
    grid = [(r, i, j) for r in range(n_rec) for i in range(n_row) for j in range(n_col)]
    to_cols = [(owner(r, n_row * j + i), device(r, i, j)) for r, i, j in grid]
    to_rows = [
        (owner((j // per) ^ r ^ (i % 2), (r * n_row + i) * per + j % per), device(r, i, j))
        for r, i, j in grid
    ]
    direct = n_col <= 4 and n_rec == low_rec
    got = flipped(send, n_col, count)
    piece = after(piece, got)
    pcols = lax.ppermute(piece, AXES, to_cols)
    prows = lax.ppermute(piece, AXES, to_rows)
    pieces = call(add_kernel, [shape((2, block, block), F32)] * half, [keep, got])
    total = sum([flipped(pieces[j], 2 * j * n_col, count) for j in range(1, half)], pieces[0])
    for bit in range(1, n_rec // low_rec):
        if bit & (bit - 1) == 0:
            total = total + flipped(total, bit * low_rec * n_row * n_col, count)
    if direct:
        parts = [flipped(total, m, count) for m in range(1, n_col)]
        pcols = after(pcols, parts[0])
        pcols = [pcols] + [flipped(pcols, 2 * j * n_col, count) for j in range(1, half)]
        total = sum(parts, total)
    else:
        total = lax.psum(total, "col")
    evens = [total] + [flipped(total, 2 * j * n_col, count) for j in range(1, half)]
    if direct:
        prows = after(prows, evens[1])
        prows = [prows] + [flipped(prows, m, count) for m in range(1, n_col)]
        others = [flipped(x, n_col, count) for x in pcols]
        pcols = [x for pair in zip(pcols, others) for x in pair]
        cols_me, rows_me = me, col
    else:
        pcols = list(lax.all_gather(pcols, ("rec", "row"), axis=0))
        prows = list(lax.all_gather(prows, "col", axis=0))
        cols_me = rows_me = jnp.int32(0)
    odds = [flipped(x, n_col, count) for x in evens]
    tri = [x for pair in zip(evens, odds) for x in pair]

    inverses, lows = call(
        lambda ids_ref, *refs: chain_kernel(ids_ref[0], *refs),
        [
            shape((PBLK, block, block), F32),
            shape((len(couplings_of(PBLK)), block, block), F32),
        ],
        [ids, *tri],
        [pltpu.VMEM((PBLK, 2, block, block), F32)],
        scalars=1,
    )
    wide = trailing_block.shape[0] + trailing_block.shape[1]
    key = jnp.stack([cols_me, rows_me]).astype(jnp.int32)

    def final_body(key_ref, *refs):
        final_kernel(key_ref[0], key_ref[1], n_row, per, len(pcols), *refs)

    return call(
        final_body,
        shape(trailing_block.shape, F32),
        [key, inverses, lows, *pcols, *prows, trailing_block],
        [pltpu.VMEM((PBLK * block, wide), F32), pltpu.VMEM((PBLK * block, wide), BF16)],
        scalars=1,
    )


def solution(mesh):
    return jax.shard_map(
        body,
        mesh=mesh,
        in_specs=(
            P(("rec", "row", "col"), None, None),
            P(("rec", "row", "col"), None, None),
            P(("rec", "row", "col"), None),
            P(("rec", "row", "col")),
            P(("rec", "row", "col")),
            P(("rec", "row"), "col"),
        ),
        out_specs=P(("rec", "row"), "col"),
        check_vma=False,
    )
```

```python
import functools

import jax
import jax.numpy as jnp
from jax import lax
from jax.experimental import pallas as pl
from jax.experimental.pallas import tpu as pltpu
from jax.sharding import PartitionSpec as P

PBLK = 8
AXES = ("rec", "row", "col")
F32 = jnp.float32
BF16 = jnp.bfloat16
SUB = 8
TAIL = 16
EARLY = 2
VMEM_BYTES = 40 * 1024 * 1024

ROWS_BY_ROWS = (((0,), (0,)), ((), ()))
COLS_BY_COLS = (((1,), (1,)), ((), ()))
PLAIN = (((1,), (0,)), ((), ()))


def split(x):
    if x.dtype == BF16:
        return x, None
    high = x.astype(BF16)
    return high, (x - high.astype(F32)).astype(BF16)


def dot3(a, b, dims):
    a_high, a_low = split(a)
    b_high, b_low = split(b)
    mul = functools.partial(lax.dot_general, dimension_numbers=dims, preferred_element_type=F32)
    out = mul(a_high, b_high)
    if b_low is not None:
        out = out + mul(a_high, b_low)
    if a_low is not None:
        out = out + mul(a_low, b_high)
    return out


def lane_copy(x, at, size):
    return jnp.broadcast_to(x[:, at : at + 1], (SUB, size))


def row_copy(x, at, size):
    return jnp.broadcast_to(x[at : at + 1, :], (SUB, size))


def tree_sum(terms):
    while len(terms) > 1:
        pairs = [terms[i] + terms[i + 1] for i in range(0, len(terms) - 1, 2)]
        terms = pairs + terms[len(terms) - len(terms) % 2 :]
    return terms[0]


def factor_step(rows, step, last, lane, sub):
    size = lane.shape[1]
    first = step * SUB
    inside = (lane >= first) & (lane < first + SUB)
    pivot_rows = [row_copy(rows[step], i, size) for i in range(SUB)]
    entry = {
        (i, j): lane_copy(pivot_rows[i], first + j, size) for i in range(SUB) for j in range(i, SUB)
    }
    below = range(step + 1, last)
    cols = {r: [lane_copy(rows[r], first + j, size) for j in range(SUB)] for r in below}
    left = [
        jnp.where(inside, jnp.where(lane == first + i, 1.0, 0.0), pivot_rows[i]) for i in range(SUB)
    ]
    recip = [None] * SUB
    for k in range(SUB):
        if k % 2 == 0:
            pivot, beside = entry[(k, k)], entry[(k, k + 1)]
            recip[k] = 1.0 / pivot
            recip[k + 1] = pivot * (1.0 / (pivot * entry[(k + 1, k + 1)] - beside * beside))
        for i in range(k + 1, SUB):
            mult = entry[(k, i)] * recip[k]
            for j in range(i, SUB):
                entry[(i, j)] = entry[(i, j)] - mult * entry[(k, j)]
            left[i] = left[i] - mult * left[k]
            for r in below:
                cols[r][i] = cols[r][i] - mult * cols[r][k]
    solved = [left[i] * recip[i] for i in range(SUB)]
    for r in below:
        part = tree_sum([cols[r][j] * solved[j] for j in range(SUB)])
        rows[r] = jnp.where(inside, 0.0, rows[r]) - part
    done = left[0] * lax.sqrt(recip[0])
    for i in range(1, SUB):
        done = jnp.where(sub == i, left[i] * lax.sqrt(recip[i]), done)
    rows[step] = done


def inverse_factors(mats, work=()):
    size = mats[0].shape[0]
    lane = lax.broadcasted_iota(jnp.int32, (SUB, size), 1)
    sub = lax.broadcasted_iota(jnp.int32, (SUB, size), 0)
    state = [[m[r : r + SUB, :] for r in range(0, size, SUB)] for m in mats]
    steps = size // SUB
    group = steps // 8 if len(mats) > 2 else steps // 2
    work = list(work)
    share = -(-len(work) // steps)
    for start in range(0, steps, group):
        stop = start + group
        for step in range(start, stop):
            for rows in state:
                factor_step(rows, step, stop, lane, sub)
            for item in work[step * share : (step + 1) * share]:
                item()
        for rows in state:
            for step in range(start, stop):
                beyond = (lane >= (step + 1) * SUB) & (lane < stop * SUB)
                rows[step] = jnp.where(beyond, 0.0, rows[step])
            if stop < steps:
                high, low = split(jnp.concatenate(rows[start:stop], axis=0))
                update = lax.dot_general(
                    jnp.concatenate([high, high, low], axis=0),
                    jnp.concatenate([high, low, high], axis=0),
                    ROWS_BY_ROWS,
                    preferred_element_type=F32,
                )
                inside = (lane >= start * SUB) & (lane < stop * SUB)
                for r in range(stop, steps):
                    rows[r] = jnp.where(inside, 0.0, rows[r]) - update[r * SUB : (r + 1) * SUB]
    out = []
    for rows in state:
        rows = [jnp.where(lane < (r + 1) * SUB, rows[r], 0.0) for r in range(steps)]
        out.append(jnp.concatenate(rows, axis=0))
    return out


def local_kernel(
    me, first_ref, count_ref, local_hbm, global_hbm, weight_hbm,
    keep_ref, send_ref, piece_ref, tri, local_ref, global_ref, weight_ref, sems,
):
    copies = [
        pltpu.make_async_copy(src, dst, sems.at[i])
        for i, (src, dst) in enumerate(
            [(weight_hbm, weight_ref), (local_hbm, local_ref), (global_hbm, global_ref)]
        )
    ]
    for copy in copies:
        copy.start()
    slots = local_ref.shape[0]
    block = local_ref.shape[2]
    tri[...] = jnp.zeros_like(tri)
    dot = functools.partial(
        lax.dot_general, dimension_numbers=ROWS_BY_ROWS, preferred_element_type=F32
    )
    copies[0].wait()
    root = jnp.sqrt(weight_ref[...])
    root = jnp.transpose(jnp.concatenate([root] * (SUB // slots), axis=0))
    copies[1].wait()
    cols = [root[:, b : b + 1] for b in range(slots)]
    locs = [(cols[b] * local_ref[b].astype(F32)).astype(BF16) for b in range(slots)]
    grams = [dot(loc, loc) for loc in locs]
    copies[2].wait()
    crosses, panels = [], []
    for b in range(slots):
        glo = (cols[b] * global_ref[b].astype(F32)).astype(BF16)
        crosses.append(dot(locs[b], glo))
        panels.append(dot(glo[:, : 2 * block], glo))
    inverses = inverse_factors(grams)
    for b in range(slots):
        white = dot3(inverses[b], crosses[b], PLAIN)
        reduced = panels[b] - dot3(white[:, : 2 * block], white, ROWS_BY_ROWS)
        live = jnp.where(count_ref[0] > b, 1.0, 0.0)
        reduced = reduced * live
        k = first_ref[b]
        one = lax.bitwise_xor(k, me)
        two = lax.bitwise_xor(k + 1, me)
        tri[one, 0] += reduced[:block, :block]
        tri[two, 0] += reduced[block:, block : 2 * block]
        tri[two, 1] += reduced[block:, :block]
        piece_ref[b, : 2 * block, :] = reduced[:, 2 * block :].astype(BF16)
        tail = jnp.broadcast_to(k.astype(F32), (TAIL, block))
        piece_ref[b, 2 * block :, :] = tail.astype(BF16)
    half = PBLK // 2
    for j in range(half):
        keep_ref[j] = tri[2 * j]
        send_ref[j] = tri[2 * j + 1]


def add_kernel(a_ref, b_ref, *out_refs):
    for j, ref in enumerate(out_refs):
        ref[...] = a_ref[j] + b_ref[j]


def levels_of(count):
    left = list(range(count))
    levels = []
    while left:
        gone = left[0::2] if len(left) > 1 else left
        level = []
        for k in gone:
            at = left.index(k)
            before = left[at - 1] if at > 0 else None
            after = left[at + 1] if at + 1 < len(left) else None
            level.append((k, before, after))
        levels.append(level)
        left = [k for k in left if k not in gone]
    return levels


def eliminate(level, diag, off, work):
    inverses = inverse_factors([diag[k] for k, _, _ in level], work)
    lows = {}
    for (k, before, after), inv in zip(level, inverses):
        if before is not None:
            low_b = dot3(inv, off[(k, before)], PLAIN)
            lows[(k, before)] = low_b
            diag[before] = diag[before] - dot3(low_b, low_b, ROWS_BY_ROWS)
        if after is not None:
            low_a = dot3(off[(after, k)], inv, COLS_BY_COLS)
            lows[(k, after)] = low_a
            diag[after] = diag[after] - dot3(low_a, low_a, COLS_BY_COLS)
        if before is not None and after is not None:
            off[(after, before)] = -dot3(low_a, low_b, PLAIN)
    return {k: inv for (k, _, _), inv in zip(level, inverses)}, lows


def early_layout():
    levels = levels_of(PBLK)
    early, late = levels[:EARLY], levels[EARLY:]
    invs = [k for level in early for k, _, _ in level]
    lows = [
        (k, n) for level in early for k, before, after in level for n in (before, after) if n is not None
    ]
    left = sorted(k for level in late for k, _, _ in level)
    return invs, lows, left, list(zip(left[1:], left[:-1]))


def factor_kernel(me, *refs):
    pieces = refs[:PBLK]
    inv_ref, low_ref, left_ref, tri = refs[PBLK:]
    for j in range(PBLK):
        tri[lax.bitwise_xor(me, j)] = pieces[j][...]
    diag = {k: tri[k, 0] for k in range(PBLK)}
    off = {(k, k - 1): tri[k, 1] for k in range(1, PBLK)}
    invs, lows, left, links = early_layout()
    for level in levels_of(PBLK)[:EARLY]:
        new_invs, new_lows = eliminate(level, diag, off, ())
        for k, value in new_invs.items():
            inv_ref[invs.index(k)] = value
        for key, value in new_lows.items():
            low_ref[lows.index(key)] = value
    for i, k in enumerate(left):
        left_ref[i] = diag[k]
    for i, key in enumerate(links):
        left_ref[len(left) + i] = off[key]


def panel_kernel(cols_me, rows_me, n_row, per, n_cols, inv_ref, low_ref, left_ref, *refs):
    terms, (trail_ref, out_ref, panel, solved) = refs[:-4], refs[-4:]
    slots, height, block = terms[0].shape
    height = height - TAIL
    tile_rows = trail_ref.shape[0]

    def place(n, b):
        if n < n_cols:
            over = tile_rows + lax.rem(lax.bitwise_xor(cols_me, n), n_row) * block
        else:
            over = lax.rem(lax.bitwise_xor(rows_me, n - n_cols), per) * block
        over = pl.multiple_of(over, block)
        term = terms[n]
        k = jnp.max(term[b, height:, :].astype(F32)).astype(jnp.int32)
        down = pl.multiple_of(k * block, block)
        panel[pl.ds(down, height), pl.ds(over, block)] += term[b, :height, :].astype(F32)

    def rows_of(k):
        return pl.ds(k * block, block)

    def solve(k, inv):
        value = dot3(inv[...], panel[rows_of(k), :], PLAIN)
        panel[rows_of(k), :] = value
        solved[rows_of(k), :] = value.astype(BF16)

    def couple(k, n, low):
        dims = PLAIN if n > k else ROWS_BY_ROWS
        panel[rows_of(n), :] -= dot3(low[...], panel[rows_of(k), :], dims)

    def solve_level(level, inverses, lows):
        items = []
        for k, before, after in level:
            items.append(functools.partial(solve, k, inverses[k]))
            for n in (before, after):
                if n is not None:
                    items.append(functools.partial(couple, k, n, lows[(k, n)]))
        return items

    panel[...] = jnp.zeros_like(panel)
    invs, lows, left, links = early_layout()
    early_invs = {k: inv_ref.at[i] for i, k in enumerate(invs)}
    early_lows = {key: low_ref.at[i] for i, key in enumerate(lows)}
    diag = {k: left_ref[i] for i, k in enumerate(left)}
    off = {key: left_ref[len(left) + i] for i, key in enumerate(links)}
    levels = levels_of(PBLK)
    work = [functools.partial(place, n, b) for n in range(len(terms)) for b in range(slots)]
    for level in levels[:EARLY]:
        work += solve_level(level, early_invs, early_lows)
    for level in levels[EARLY:]:
        new_invs, new_lows = eliminate(level, diag, off, work)
        work = solve_level(level, new_invs, new_lows)
    for item in work:
        item()
    update = lax.dot_general(
        solved[:, :tile_rows], solved[:, tile_rows:], ROWS_BY_ROWS, preferred_element_type=F32
    )
    out_ref[...] = trail_ref[...] - update


VMEM = pl.BlockSpec(memory_space=pltpu.VMEM)
SMEM = pl.BlockSpec(memory_space=pltpu.SMEM)
HBM = pl.BlockSpec(memory_space=pltpu.HBM)
PARAMS = pltpu.CompilerParams(vmem_limit_bytes=VMEM_BYTES)


def call(kernel, out_shape, ins, scratch=(), scalars=0, hbm=()):
    return pl.pallas_call(
        kernel,
        out_shape=out_shape,
        in_specs=[SMEM if i < scalars else HBM if i in hbm else VMEM for i in range(len(ins))],
        out_specs=jax.tree.map(lambda _: VMEM, out_shape),
        scratch_shapes=scratch,
        compiler_params=PARAMS,
    )(*ins)


def after(x, *others):
    return lax.optimization_barrier((x, others))[0]


def flipped(x, mask, count):
    return lax.ppermute(x, AXES, [(i, i ^ mask) for i in range(count)])


def body(local_derivs, global_derivs, weights, first_block, bundle_count, trailing_block):
    n_rec, n_row, n_col = (lax.axis_size(a) for a in AXES)
    count = n_rec * n_row * n_col
    rec, row, col = (lax.axis_index(a) for a in AXES)
    block = local_derivs.shape[2]
    half = PBLK // 2
    low_rec = PBLK // n_row
    me = row + n_row * lax.rem(rec, low_rec)
    ids = jnp.reshape(me, (1,)).astype(jnp.int32)
    shape = jax.ShapeDtypeStruct
    slots, height = local_derivs.shape[0], 2 * block + TAIL
    keep, send, piece = call(
        lambda ids_ref, *refs: local_kernel(ids_ref[0], *refs),
        [
            shape((half, 2, block, block), F32),
            shape((half, 2, block, block), F32),
            shape((slots, height, block), BF16),
        ],
        [ids, first_block, bundle_count, local_derivs, global_derivs, weights],
        [
            pltpu.VMEM((PBLK, 2, block, block), F32),
            pltpu.VMEM(local_derivs.shape, BF16),
            pltpu.VMEM(global_derivs.shape, BF16),
            pltpu.VMEM(weights.shape, F32),
            pltpu.SemaphoreType.DMA((3,)),
        ],
        scalars=3,
        hbm=(3, 4, 5),
    )
    per = n_col // n_rec
    owner = lambda r, c: (r * n_row + c // n_col) * n_col + c % n_col
    device = lambda r, i, j: (r * n_row + i) * n_col + j
    grid = [(r, i, j) for r in range(n_rec) for i in range(n_row) for j in range(n_col)]
    to_cols = [(owner(r, n_row * j + i), device(r, i, j)) for r, i, j in grid]
    to_rows = [
        (owner((j // per) ^ r ^ (i % 2), (r * n_row + i) * per + j % per), device(r, i, j))
        for r, i, j in grid
    ]
    direct = n_col <= 4 and n_rec == low_rec
    got = flipped(send, n_col, count)
    piece = after(piece, got)
    pcols = lax.ppermute(piece, AXES, to_cols)
    prows = lax.ppermute(piece, AXES, to_rows)
    pieces = call(add_kernel, [shape((2, block, block), F32)] * half, [keep, got])
    total = sum([flipped(pieces[j], 2 * j * n_col, count) for j in range(1, half)], pieces[0])
    for bit in range(1, n_rec // low_rec):
        if bit & (bit - 1) == 0:
            total = total + flipped(total, bit * low_rec * n_row * n_col, count)
    if direct:
        total = sum([flipped(total, m, count) for m in range(1, n_col)], total)
    else:
        total = lax.psum(total, "col")
    evens = [total] + [flipped(total, 2 * j * n_col, count) for j in range(1, half)]
    pcols, prows = after((pcols, prows), evens)
    odds = [flipped(x, n_col, count) for x in evens]
    tri = [x for pair in zip(evens, odds) for x in pair]
    if direct:
        pcols = [pcols] + [flipped(pcols, 2 * j * n_col, count) for j in range(1, half)]
        prows = [prows] + [flipped(prows, m, count) for m in range(1, n_col)]
        cols_me, rows_me = me, col
    else:
        pcols = list(lax.all_gather(pcols, ("rec", "row"), axis=0))
        prows = list(lax.all_gather(prows, "col", axis=0))
        cols_me = rows_me = jnp.int32(0)
    wide = trailing_block.shape[0] + trailing_block.shape[1]
    key = jnp.stack([me, cols_me, rows_me]).astype(jnp.int32)
    invs, lows, left, links = early_layout()
    early = call(
        lambda key_ref, *refs: factor_kernel(key_ref[0], *refs),
        [shape((n, block, block), F32) for n in (len(invs), len(lows), len(left) + len(links))],
        [key, *tri],
        [pltpu.VMEM((PBLK, 2, block, block), F32)],
        scalars=1,
    )
    if direct:
        pcols = after(pcols, early)
        others = [flipped(x, n_col, count) for x in pcols]
        pcols = [x for pair in zip(pcols, others) for x in pair]

    def panel_body(key_ref, *refs):
        panel_kernel(key_ref[1], key_ref[2], n_row, per, len(pcols), *refs)

    return call(
        panel_body,
        shape(trailing_block.shape, F32),
        [key, *early, *pcols, *prows, trailing_block],
        [pltpu.VMEM((PBLK * block, wide), F32), pltpu.VMEM((PBLK * block, wide), BF16)],
        scalars=1,
    )


def solution(mesh):
    return jax.shard_map(
        body,
        mesh=mesh,
        in_specs=(
            P(("rec", "row", "col"), None, None),
            P(("rec", "row", "col"), None, None),
            P(("rec", "row", "col"), None),
            P(("rec", "row", "col")),
            P(("rec", "row", "col")),
            P(("rec", "row"), "col"),
        ),
        out_specs=P(("rec", "row"), "col"),
        check_vma=False,
    )
```

```python
import functools

import jax
import jax.numpy as jnp
from jax import lax
from jax.experimental import pallas as pl
from jax.experimental.pallas import tpu as pltpu
from jax.sharding import PartitionSpec as P

PBLK = 8
AXES = ("rec", "row", "col")
F32 = jnp.float32
BF16 = jnp.bfloat16
SUB = 8
TAIL = 16
CUT = 3
FLOPS_PER_MICRO = 10**9
BYTES_PER_MICRO = 3 * 10**6
VMEM_BYTES = 40 * 1024 * 1024

ROWS_BY_ROWS = (((0,), (0,)), ((), ()))
COLS_BY_COLS = (((1,), (1,)), ((), ()))
PLAIN = (((1,), (0,)), ((), ()))


def split(x):
    if x.dtype == BF16:
        return x, None
    high = x.astype(BF16)
    return high, (x - high.astype(F32)).astype(BF16)


def dot3(a, b, dims):
    a_high, a_low = split(a)
    b_high, b_low = split(b)
    mul = functools.partial(lax.dot_general, dimension_numbers=dims, preferred_element_type=F32)
    out = mul(a_high, b_high)
    if b_low is not None:
        out = out + mul(a_high, b_low)
    if a_low is not None:
        out = out + mul(a_low, b_high)
    return out


def lane_copy(x, at, size):
    return jnp.broadcast_to(x[:, at : at + 1], (SUB, size))


def row_copy(x, at, size):
    return jnp.broadcast_to(x[at : at + 1, :], (SUB, size))


def tree_sum(terms):
    while len(terms) > 1:
        pairs = [terms[i] + terms[i + 1] for i in range(0, len(terms) - 1, 2)]
        terms = pairs + terms[len(terms) - len(terms) % 2 :]
    return terms[0]


def factor_step(rows, step, last, lane, sub):
    size = lane.shape[1]
    first = step * SUB
    inside = (lane >= first) & (lane < first + SUB)
    pivot_rows = [row_copy(rows[step], i, size) for i in range(SUB)]
    entry = {
        (i, j): lane_copy(pivot_rows[i], first + j, size) for i in range(SUB) for j in range(i, SUB)
    }
    below = range(step + 1, last)
    cols = {r: [lane_copy(rows[r], first + j, size) for j in range(SUB)] for r in below}
    left = [
        jnp.where(inside, jnp.where(lane == first + i, 1.0, 0.0), pivot_rows[i]) for i in range(SUB)
    ]
    recip = [None] * SUB
    for k in range(SUB):
        if k % 2 == 0:
            pivot, beside = entry[(k, k)], entry[(k, k + 1)]
            recip[k] = 1.0 / pivot
            recip[k + 1] = pivot * (1.0 / (pivot * entry[(k + 1, k + 1)] - beside * beside))
        for i in range(k + 1, SUB):
            mult = entry[(k, i)] * recip[k]
            for j in range(i, SUB):
                entry[(i, j)] = entry[(i, j)] - mult * entry[(k, j)]
            left[i] = left[i] - mult * left[k]
            for r in below:
                cols[r][i] = cols[r][i] - mult * cols[r][k]
    solved = [left[i] * recip[i] for i in range(SUB)]
    for r in below:
        part = tree_sum([cols[r][j] * solved[j] for j in range(SUB)])
        rows[r] = jnp.where(inside, 0.0, rows[r]) - part
    done = left[0] * lax.sqrt(recip[0])
    for i in range(1, SUB):
        done = jnp.where(sub == i, left[i] * lax.sqrt(recip[i]), done)
    rows[step] = done


def inverse_factors(mats, work=()):
    size = mats[0].shape[0]
    lane = lax.broadcasted_iota(jnp.int32, (SUB, size), 1)
    sub = lax.broadcasted_iota(jnp.int32, (SUB, size), 0)
    state = [[m[r : r + SUB, :] for r in range(0, size, SUB)] for m in mats]
    steps = size // SUB
    group = steps // 8 if len(mats) > 2 else steps // 2
    work = list(work)
    share = -(-len(work) // steps)
    for start in range(0, steps, group):
        stop = start + group
        for step in range(start, stop):
            for rows in state:
                factor_step(rows, step, stop, lane, sub)
            for item in work[step * share : (step + 1) * share]:
                item()
        for rows in state:
            for step in range(start, stop):
                beyond = (lane >= (step + 1) * SUB) & (lane < stop * SUB)
                rows[step] = jnp.where(beyond, 0.0, rows[step])
            if stop < steps:
                high, low = split(jnp.concatenate(rows[start:stop], axis=0))
                update = lax.dot_general(
                    jnp.concatenate([high, high, low], axis=0),
                    jnp.concatenate([high, low, high], axis=0),
                    ROWS_BY_ROWS,
                    preferred_element_type=F32,
                )
                inside = (lane >= start * SUB) & (lane < stop * SUB)
                for r in range(stop, steps):
                    rows[r] = jnp.where(inside, 0.0, rows[r]) - update[r * SUB : (r + 1) * SUB]
    out = []
    for rows in state:
        rows = [jnp.where(lane < (r + 1) * SUB, rows[r], 0.0) for r in range(steps)]
        out.append(jnp.concatenate(rows, axis=0))
    return out


def local_kernel(
    me, first_ref, count_ref, local_hbm, global_hbm, weight_hbm,
    keep_ref, send_ref, piece_ref, tri, local_ref, global_ref, weight_ref, sems,
):
    copies = [
        pltpu.make_async_copy(src, dst, sems.at[i])
        for i, (src, dst) in enumerate(
            [(weight_hbm, weight_ref), (local_hbm, local_ref), (global_hbm, global_ref)]
        )
    ]
    for copy in copies:
        copy.start()
    slots = local_ref.shape[0]
    block = local_ref.shape[2]
    tri[...] = jnp.zeros_like(tri)
    dot = functools.partial(
        lax.dot_general, dimension_numbers=ROWS_BY_ROWS, preferred_element_type=F32
    )
    copies[0].wait()
    root = jnp.sqrt(weight_ref[...])
    root = jnp.transpose(jnp.concatenate([root] * (SUB // slots), axis=0))
    copies[1].wait()
    cols = [root[:, b : b + 1] for b in range(slots)]
    locs = [(cols[b] * local_ref[b].astype(F32)).astype(BF16) for b in range(slots)]
    grams = [dot(loc, loc) for loc in locs]
    copies[2].wait()
    crosses, panels = [], []
    for b in range(slots):
        glo = (cols[b] * global_ref[b].astype(F32)).astype(BF16)
        crosses.append(dot(locs[b], glo))
        panels.append(dot(glo[:, : 2 * block], glo))
    inverses = inverse_factors(grams)
    for b in range(slots):
        white = dot3(inverses[b], crosses[b], PLAIN)
        reduced = panels[b] - dot3(white[:, : 2 * block], white, ROWS_BY_ROWS)
        live = jnp.where(count_ref[0] > b, 1.0, 0.0)
        reduced = reduced * live
        k = first_ref[b]
        one = lax.bitwise_xor(k, me)
        two = lax.bitwise_xor(k + 1, me)
        tri[one, 0] += reduced[:block, :block]
        tri[two, 0] += reduced[block:, block : 2 * block]
        tri[two, 1] += reduced[block:, :block]
        piece_ref[b, : 2 * block, :] = reduced[:, 2 * block :].astype(BF16)
        tail = jnp.broadcast_to(k.astype(F32), (TAIL, block))
        piece_ref[b, 2 * block :, :] = tail.astype(BF16)
    half = PBLK // 2
    for j in range(half):
        keep_ref[j] = tri[2 * j]
        send_ref[j] = tri[2 * j + 1]


def add_kernel(a_ref, b_ref, *out_refs):
    for j, ref in enumerate(out_refs):
        ref[...] = a_ref[j] + b_ref[j]


def levels_of(count):
    left = list(range(count))
    levels = []
    while left:
        gone = left[0::2] if len(left) > 1 else left
        level = []
        for k in gone:
            at = left.index(k)
            before = left[at - 1] if at > 0 else None
            after = left[at + 1] if at + 1 < len(left) else None
            level.append((k, before, after))
        levels.append(level)
        left = [k for k in left if k not in gone]
    return levels


def eliminate(level, diag, off, work=(), inverses=None):
    if inverses is None:
        inverses = inverse_factors([diag[k] for k, _, _ in level], work)
    lows = {}
    for (k, before, after), inv in zip(level, inverses):
        if before is not None:
            low_b = dot3(inv, off[(k, before)], PLAIN)
            lows[(k, before)] = low_b
            diag[before] = diag[before] - dot3(low_b, low_b, ROWS_BY_ROWS)
        if after is not None:
            low_a = dot3(off[(after, k)], inv, COLS_BY_COLS)
            lows[(k, after)] = low_a
            diag[after] = diag[after] - dot3(low_a, low_a, COLS_BY_COLS)
        if before is not None and after is not None:
            off[(after, before)] = -dot3(low_a, low_b, PLAIN)
    return {k: inv for (k, _, _), inv in zip(level, inverses)}, lows


def layout():
    levels = levels_of(PBLK)
    invs = [k for level in levels[:CUT] for k, _, _ in level]
    lows = [
        (k, n) for level in levels[:CUT] for k, before, after in level for n in (before, after) if n is not None
    ]
    left = sorted(k for level in levels[CUT:] for k, _, _ in level)
    return invs, lows, left, list(zip(left[1:], left[:-1]))


def own_kernel(me, *refs):
    *parts, out_ref = refs
    diag = tree_sum([part[0] for part in parts])
    out_ref[1] = tree_sum([part[1] for part in parts])
    inverse = inverse_factors([diag])[0]
    out_ref[0] = jnp.where(lax.rem(me, 2) == 0, inverse, diag)


def factor_kernel(me, *refs):
    pieces = refs[:PBLK]
    inv_ref, low_ref, left_ref, tri = refs[PBLK:]
    for j in range(PBLK):
        tri[lax.bitwise_xor(me, j)] = pieces[j][...]
    diag = {k: tri[k, 0] for k in range(PBLK)}
    off = {(k, k - 1): tri[k, 1] for k in range(1, PBLK)}
    invs, lows, left, links = layout()
    levels = levels_of(PBLK)[:CUT]
    given = [diag[k] for k, _, _ in levels[0]]
    for level, inverses in zip(levels, [given] + [None] * (CUT - 1)):
        new_invs, new_lows = eliminate(level, diag, off, inverses=inverses)
        for k, value in new_invs.items():
            inv_ref[invs.index(k)] = value
        for key, value in new_lows.items():
            low_ref[lows.index(key)] = value
    for i, k in enumerate(left):
        left_ref[i] = diag[k]
    for i, key in enumerate(links):
        left_ref[len(left) + i] = off[key]


def panel_kernel(cols_me, rows_me, n_row, per, n_cols, *refs):
    (inv_ref, low_ref, left_ref), refs = refs[:3], refs[3:]
    terms, (trail_ref, out_ref, panel, solved) = refs[:-4], refs[-4:]
    slots, height, block = terms[0].shape
    height = height - TAIL
    tile_rows = trail_ref.shape[0]

    def place(n, b):
        if n < n_cols:
            over = tile_rows + lax.rem(lax.bitwise_xor(cols_me, n), n_row) * block
        else:
            over = lax.rem(lax.bitwise_xor(rows_me, n - n_cols), per) * block
        over = pl.multiple_of(over, block)
        term = terms[n]
        k = jnp.max(term[b, height:, :].astype(F32)).astype(jnp.int32)
        down = pl.multiple_of(k * block, block)
        panel[pl.ds(down, height), pl.ds(over, block)] += term[b, :height, :].astype(F32)

    def rows_of(k):
        return pl.ds(k * block, block)

    def solve(k, inv):
        value = dot3(inv[...], panel[rows_of(k), :], PLAIN)
        panel[rows_of(k), :] = value
        solved[rows_of(k), :] = value.astype(BF16)

    def couple(k, n, low):
        dims = PLAIN if n > k else ROWS_BY_ROWS
        panel[rows_of(n), :] -= dot3(low[...], panel[rows_of(k), :], dims)

    def solve_level(level, inverses, lows):
        items = []
        for k, before, after in level:
            items.append(functools.partial(solve, k, inverses[k]))
            for n in (before, after):
                if n is not None:
                    items.append(functools.partial(couple, k, n, lows[(k, n)]))
        return items

    panel[...] = jnp.zeros_like(panel)
    levels = levels_of(PBLK)
    work = [functools.partial(place, n, b) for n in range(len(terms)) for b in range(slots)]
    invs, lows, left, links = layout()
    early_invs = {k: inv_ref.at[i] for i, k in enumerate(invs)}
    early_lows = {key: low_ref.at[i] for i, key in enumerate(lows)}
    for level in levels[:CUT]:
        work += solve_level(level, early_invs, early_lows)
    diag = {k: left_ref[i] for i, k in enumerate(left)}
    off = {key: left_ref[len(left) + i] for i, key in enumerate(links)}
    for level in levels[CUT:]:
        new_invs, new_lows = eliminate(level, diag, off, work)
        work = solve_level(level, new_invs, new_lows)
    for item in work:
        item()
    update = lax.dot_general(
        solved[:, :tile_rows], solved[:, tile_rows:], ROWS_BY_ROWS, preferred_element_type=F32
    )
    out_ref[...] = trail_ref[...] - update


VMEM = pl.BlockSpec(memory_space=pltpu.VMEM)
SMEM = pl.BlockSpec(memory_space=pltpu.SMEM)
HBM = pl.BlockSpec(memory_space=pltpu.HBM)
PARAMS = pltpu.CompilerParams(vmem_limit_bytes=VMEM_BYTES)


def call(kernel, out_shape, ins, scratch=(), scalars=0, hbm=(), micros=1):
    return pl.pallas_call(
        kernel,
        out_shape=out_shape,
        in_specs=[SMEM if i < scalars else HBM if i in hbm else VMEM for i in range(len(ins))],
        out_specs=jax.tree.map(lambda _: VMEM, out_shape),
        scratch_shapes=scratch,
        compiler_params=PARAMS,
        cost_estimate=pl.CostEstimate(
            flops=micros * FLOPS_PER_MICRO, bytes_accessed=micros * BYTES_PER_MICRO, transcendentals=0
        ),
    )(*ins)


def after(x, *others):
    return lax.optimization_barrier((x, others))[0]


def flipped(x, mask, count):
    return lax.ppermute(x, AXES, [(i, i ^ mask) for i in range(count)])


def body(local_derivs, global_derivs, weights, first_block, bundle_count, trailing_block):
    n_rec, n_row, n_col = (lax.axis_size(a) for a in AXES)
    count = n_rec * n_row * n_col
    rec, row, col = (lax.axis_index(a) for a in AXES)
    block = local_derivs.shape[2]
    half = PBLK // 2
    low_rec = PBLK // n_row
    me = row + n_row * lax.rem(rec, low_rec)
    ids = jnp.reshape(me, (1,)).astype(jnp.int32)
    shape = jax.ShapeDtypeStruct
    slots, height = local_derivs.shape[0], 2 * block + TAIL
    keep, send, piece = call(
        lambda ids_ref, *refs: local_kernel(ids_ref[0], *refs),
        [
            shape((half, 2, block, block), F32),
            shape((half, 2, block, block), F32),
            shape((slots, height, block), BF16),
        ],
        [ids, first_block, bundle_count, local_derivs, global_derivs, weights],
        [
            pltpu.VMEM((PBLK, 2, block, block), F32),
            pltpu.VMEM(local_derivs.shape, BF16),
            pltpu.VMEM(global_derivs.shape, BF16),
            pltpu.VMEM(weights.shape, F32),
            pltpu.SemaphoreType.DMA((3,)),
        ],
        scalars=3,
        hbm=(3, 4, 5),
    )
    per = n_col // n_rec
    owner = lambda r, c: (r * n_row + c // n_col) * n_col + c % n_col
    device = lambda r, i, j: (r * n_row + i) * n_col + j
    grid = [(r, i, j) for r in range(n_rec) for i in range(n_row) for j in range(n_col)]
    to_cols = [(owner(r, n_row * j + i), device(r, i, j)) for r, i, j in grid]
    to_rows = [
        (owner((j // per) ^ r ^ (i % 2), (r * n_row + i) * per + j % per), device(r, i, j))
        for r, i, j in grid
    ]
    direct = n_col <= 4 and n_rec == low_rec
    got = flipped(send, n_col, count)
    pcols = lax.ppermute(piece, AXES, to_cols)
    pieces = call(add_kernel, [shape((2, block, block), F32)] * half, [keep, got])
    total = sum([flipped(pieces[j], 2 * j * n_col, count) for j in range(1, half)], pieces[0])
    total, pcols = lax.optimization_barrier((total, pcols))
    for bit in range(1, n_rec // low_rec):
        if bit & (bit - 1) == 0:
            total = total + flipped(total, bit * low_rec * n_row * n_col, count)
    if direct:
        parts = [total] + [flipped(total, m, count) for m in range(1, n_col)]
    else:
        parts = [lax.psum(total, "col")]
    if direct:
        pcols = [pcols] + [flipped(pcols, 2 * j * n_col, count) for j in range(1, half)]
    else:
        pcols = list(lax.all_gather(pcols, ("rec", "row"), axis=0))
    pcols, parts, piece = lax.optimization_barrier((pcols, parts, piece))
    prows = lax.ppermute(piece, AXES, to_rows)
    own = call(
        lambda ids_ref, *refs: own_kernel(ids_ref[0], *refs),
        shape((2, block, block), F32),
        [ids, *parts],
        scalars=1,
        micros=4,
    )
    evens = [own] + [flipped(own, 2 * j * n_col, count) for j in range(1, half)]
    prows = after(prows, evens)
    odds = [flipped(x, n_col, count) for x in evens]
    tri = [x for pair in zip(evens, odds) for x in pair]
    if direct:
        prows = [prows] + [flipped(prows, m, count) for m in range(1, n_col)]
        cols_me, rows_me = me, col
    else:
        prows = list(lax.all_gather(prows, "col", axis=0))
        cols_me = rows_me = jnp.int32(0)
    wide = trailing_block.shape[0] + trailing_block.shape[1]
    key = jnp.stack([me, cols_me, rows_me]).astype(jnp.int32)
    invs, lows, left, links = layout()
    early = call(
        lambda key_ref, *refs: factor_kernel(key_ref[0], *refs),
        [shape((n, block, block), F32) for n in (len(invs), len(lows), len(left) + len(links))],
        [key, *tri],
        [pltpu.VMEM((PBLK, 2, block, block), F32)],
        scalars=1,
        micros=12,
    )
    if direct:
        pcols = after(pcols, early)
        others = [flipped(x, n_col, count) for x in pcols]
        pcols = [x for pair in zip(pcols, others) for x in pair]

    def panel_body(key_ref, *refs):
        panel_kernel(key_ref[1], key_ref[2], n_row, per, len(pcols), *refs)

    return call(
        panel_body,
        shape(trailing_block.shape, F32),
        [key, *early, *pcols, *prows, trailing_block],
        [pltpu.VMEM((PBLK * block, wide), F32), pltpu.VMEM((PBLK * block, wide), BF16)],
        scalars=1,
    )


def solution(mesh):
    return jax.shard_map(
        body,
        mesh=mesh,
        in_specs=(
            P(("rec", "row", "col"), None, None),
            P(("rec", "row", "col"), None, None),
            P(("rec", "row", "col"), None),
            P(("rec", "row", "col")),
            P(("rec", "row", "col")),
            P(("rec", "row"), "col"),
        ),
        out_specs=P(("rec", "row"), "col"),
        check_vma=False,
    )
```
